1024 devices in a mesh: sy: 16 (over y, core), sz: 16 (over z), traj: 4 (over x).
Axes of the slice: x: 4, y: 8, z: 16, core: 2. Of those that a mesh axis runs over, the one named last changes fastest.
Arguments:
- coeffs: float32 [512, 256], P('traj'), may hold values from -6 to 6
- basis: bfloat16 [256, 64, 64, 128], P(None, 'sy', 'sz'), may hold values from -0.375 to 0.375
- damping: float32 [256], replicated, may hold values from 0.2 to 2
- w_in: float32 [8, 7], replicated, may hold values from -3 to 3
- b_in: float32 [8], replicated, may hold values from -3 to 3
- w_out: float32 [8], replicated, may hold values from -2 to 2
Outputs:
- tendency: float32 [512, 256], P('traj')
The draws below stay inside these ranges and needn't reach their ends.
All inputs are finite; a program needn't handle non-finite values.
Results may differ from the reference program's by a relative error of at most 0.0072.
Values may be sent and summed in bfloat16 or wider, within the bound.
A program may use at most 32 MiB of HBM per device.

```python
import math
import jax
import jax.numpy as jnp
from jax import lax

R = 256
HID = 8
NY = 128
NX = 64
NZ = 64
TRAJ = 512


def block_scale(key, shape, shards, least, high):
    loudness = 1.0
    for dim, blocks in shards:
        steps = jax.random.uniform(jax.random.fold_in(jax.random.fold_in(key, 6), dim), (blocks,), jnp.float32, least / len(shards), high / len(shards))
        loudness = loudness * jnp.repeat(jnp.exp(steps), shape[dim] // blocks).reshape((-1,) + (1,) * (len(shape) - 1 - dim))
    return loudness


def noise(stream_key, shape, scale, bound, split=(), dtype=jnp.bfloat16):
    loudness = block_scale(stream_key, shape, split, -0.22, 0.18) if split else 1.0
    drawn = jax.random.normal(stream_key, shape, jnp.float32) * scale * loudness
    return jnp.minimum(jnp.maximum(drawn, -bound), bound).astype(dtype)


def setup_inputs(seed: int = 0) -> dict:
    key_of = jax.random.split(jax.random.key(seed), 7)
    return {
        "coeffs": noise(key_of[0], (TRAJ, R), 1.0, 6.0, ((0, 4),), jnp.float32),
        "basis": noise(key_of[1], (R, NX, NZ, NY), R ** -0.5, 0.375, ((1, 16), (2, 16))),
        "damping": jnp.clip(jnp.exp(jax.random.uniform(key_of[2], (R,), jnp.float32, math.log(0.2), math.log(2.0))), 0.2, 2.0),
        "w_in": noise(key_of[3], (HID, 7), 0.5, 3.0, (), jnp.float32),
        "b_in": noise(key_of[4], (HID,), 0.5, 3.0, (), jnp.float32),
        "w_out": noise(key_of[5], (HID,), HID ** -0.5, 2.0, (), jnp.float32),
    }


def closure_of(field, w_in, b_in, w_out):
    padded = jnp.pad(field, ((0, 0), (1, 1), (1, 1), (1, 1)))
    center = padded[:, 1:-1, 1:-1, 1:-1]
    taps = (center,
            padded[:, :-2, 1:-1, 1:-1], padded[:, 2:, 1:-1, 1:-1],
            padded[:, 1:-1, 1:-1, :-2], padded[:, 1:-1, 1:-1, 2:],
            padded[:, 1:-1, :-2, 1:-1], padded[:, 1:-1, 2:, 1:-1])
    total = jnp.zeros(center.shape, jnp.float32)
    for hidden in range(HID):
        inner = b_in[hidden] + w_in[hidden, 0] * taps[0]
        for index in range(1, 7):
            inner = inner + w_in[hidden, index] * taps[index]
        total = total + w_out[hidden] * jnp.tanh(inner)
    return total


def reference(coeffs, basis, damping, w_in, b_in, w_out):
    flat = basis.reshape(R, NX * NZ * NY)
    scale = (R / (NX * NY * NZ)) ** 0.5
    block = 8

    def project(state_block):
        state_b = state_block.astype(jnp.bfloat16)
        field = jnp.dot(state_b, flat, preferred_element_type=jnp.float32).reshape(block, NX, NZ, NY)
        closure = closure_of(field, w_in, b_in, w_out).astype(jnp.bfloat16)
        return lax.dot_general(closure.reshape(block, NX * NZ * NY), flat, (((1,), (1,)), ((), ())), preferred_element_type=jnp.float32)

    def rate(state):
        modal = lax.map(project, state.reshape(TRAJ // block, block, R)).reshape(TRAJ, R)
        return -damping * state + scale * modal

    first = rate(coeffs)
    second = rate(coeffs + 0.5 * first)
    return 0.5 * (first + second)
```

```python
import functools
import jax
import jax.numpy as jnp
from jax import lax
from jax.experimental import pallas as pl
from jax.experimental.pallas import tpu as pltpu
from jax.sharding import PartitionSpec as P

f32, bf16 = jnp.float32, jnp.bfloat16
MESH = pl.DeviceIdType.MESH
CHUNK = 64


def kernel(
    ny, nz, scale,
    coeffs_ref, damping_ref, w_in, b_in, w_out, basis_hbm,
    out_ref,
    raw, own, halo_y, halo_z, field, left, right, clos,
    state0, state1, result,
    part_f, part_b, in_y, sum_y, in_z, row_out, rows_all, piece,
    raw_sem, halo_send, halo_recv, send_sem, recv_sem,
):
    ns = 2 * ny
    batch, modes = coeffs_ref.shape
    half = modes // 2
    per_y = batch // ny
    per_z = per_y // nz
    sy, sz = lax.axis_index("sy"), lax.axis_index("sz")
    my_y, my_core = sy // 2, lax.rem(sy, 2)

    barrier = pltpu.get_barrier_semaphore()

    def greet_y(d, _):
        pl.semaphore_signal(barrier, inc=1, device_id={"sy": lax.rem(sy + d, ns)}, device_id_type=MESH)
        return 0

    def greet_z(d, _):
        pl.semaphore_signal(barrier, inc=1, device_id={"sz": lax.rem(sz + d, nz)}, device_id_type=MESH)
        return 0

    lax.fori_loop(1, ns, greet_y, 0)
    lax.fori_loop(1, nz, greet_z, 0)

    load = pltpu.make_async_copy(basis_hbm, raw, raw_sem)
    load.start()
    coeffs = coeffs_ref[...]
    state0[0] = coeffs[:, :half].astype(bf16)
    state0[1] = coeffs[:, half:].astype(bf16)
    source = lax.broadcasted_iota(jnp.int32, (256, 256), 1)
    target = lax.broadcasted_iota(jnp.int32, (256, 256), 0)
    perm = jnp.where(
        (lax.shift_right_logical(target, 4) == (source & 15))
        & ((target & 15) == lax.shift_right_logical(source, 4)),
        1.0, 0.0,
    ).astype(bf16)
    load.wait()
    for block in range(16):
        moved = jnp.dot(
            perm, raw[block * 256:(block + 1) * 256, :], preferred_element_type=f32
        ).astype(bf16)
        for cell in range(16):
            own[cell // 4, cell % 4, block * 16:(block + 1) * 16, :] = moved[cell * 16:(cell + 1) * 16]

    pl.semaphore_wait(barrier, ns + nz - 2)

    y_next, y_prev = lax.rem(sy + 1, ns), lax.rem(sy + ns - 1, ns)
    z_next, z_prev = lax.rem(sz + 1, nz), lax.rem(sz + nz - 1, nz)
    halos = []
    for slot, (src, dst, where) in enumerate((
        (own.at[:, 3], halo_z.at[0], {"sz": z_next}),
        (own.at[:, 0], halo_z.at[1], {"sz": z_prev}),
        (own.at[3], halo_y.at[0], {"sy": y_next}),
        (own.at[0], halo_y.at[1], {"sy": y_prev}),
    )):
        copy = pltpu.make_async_remote_copy(
            src_ref=src, dst_ref=dst, send_sem=halo_send.at[slot], recv_sem=halo_recv.at[slot],
            device_id=where, device_id_type=MESH,
        )
        copy.start()
        halos.append(copy)

    def pair_field(state, first, second):
        lhs = jnp.concatenate([state[0], state[1]], axis=1)
        both = jnp.dot(lhs, jnp.concatenate([first, second], axis=1), preferred_element_type=f32)
        return both[:, :128], both[:, 128:]

    lane = lax.broadcasted_iota(jnp.int32, (batch, 128), 1)

    def field_own(state):
        for y in range(4):
            for z in (0, 2):
                for k, value in enumerate(pair_field(state, own[y, z], own[y, z + 1])):
                    field[y + 1, z + k + 1] = value
                    left[y, z + k] = jnp.where(lane == 0, 0.0, pltpu.roll(value, 1, 1))
                    right[y, z + k] = jnp.where(lane == 127, 0.0, pltpu.roll(value, 127, 1))

    def field_y(state):
        for side, inside in ((0, sy > 0), (1, sy < ns - 1)):
            for z in (0, 2):
                for k, value in enumerate(pair_field(state, halo_y[side, z], halo_y[side, z + 1])):
                    field[5 * side, z + k + 1] = jnp.where(inside, value, 0.0)

    def field_z(state):
        for side, inside in ((0, sz > 0), (1, sz < nz - 1)):
            for y in (0, 2):
                for k, value in enumerate(pair_field(state, halo_z[side, y], halo_z[side, y + 1])):
                    field[y + k + 1, 5 * side] = jnp.where(inside, value, 0.0)

    def closure(count, cell_of):
        chunks = batch // CHUNK

        def body(i, _):
            y, z = cell_of(i // chunks)
            at = pl.ds(pl.multiple_of(lax.rem(i, chunks) * CHUNK, CHUNK), CHUNK)
            taps = (
                field[y + 1, z + 1, at, :],
                field[y, z + 1, at, :],
                field[y + 2, z + 1, at, :],
                left[y, z, at, :],
                right[y, z, at, :],
                field[y + 1, z, at, :],
                field[y + 1, z + 2, at, :],
            )
            total = jnp.zeros((CHUNK, 128), f32)
            for h in range(8):
                inner = b_in[h] + w_in[h, 0] * taps[0]
                for k in range(1, 7):
                    inner = inner + w_in[h, k] * taps[k]
                total = total + w_out[h] * jnp.tanh(inner)
            clos[y, z, at, :] = total.astype(bf16)
            return 0

        lax.fori_loop(0, count * chunks, body, 0)

    def project(section):
        lhs = jnp.concatenate([clos[c // 4, c % 4] for c in range(16)], axis=1)
        rhs = jnp.concatenate([own[c // 4, c % 4] for c in range(16)], axis=1)
        partial = lax.dot_general(lhs, rhs, (((1,), (1,)), ((), ())), preferred_element_type=f32)
        for c in range(2):
            part_f[section, c] = partial[:, c * half:(c + 1) * half]
            part_b[section, c] = partial[:, c * half:(c + 1) * half].astype(bf16)

    def exchange(section, phase, axis, count, src_of, dst_of):
        me = sy if axis == "sy" else sz

        def copy_of(d):
            peer = lax.rem(me + d, count)
            return pltpu.make_async_remote_copy(
                src_ref=src_of(peer), dst_ref=dst_of(d),
                send_sem=send_sem.at[section, phase, d], recv_sem=recv_sem.at[section, phase, d],
                device_id={axis: peer}, device_id_type=MESH,
            )

        def start(d, _):
            copy_of(d).start()
            return 0

        def finish(d, _):
            copy_of(d).wait()
            return 0

        lax.fori_loop(1, count, start, 0)
        lax.fori_loop(1, count, finish, 0)

    rows_y = pl.ds(pl.multiple_of(my_y * per_y, per_y), per_y)

    def reduced(section):
        exchange(
            section, 0, "sy", ns,
            lambda t: part_b.at[section, lax.rem(t, 2), pl.ds(pl.multiple_of(t // 2 * per_y, per_y), per_y)],
            lambda d: in_y.at[section, d],
        )
        total = part_f[section, my_core, rows_y, :]
        for d in range(1, ns):
            total = total + in_y[section, d].astype(f32)
        for z in range(nz):
            sum_y[section, z] = total[z * per_z:(z + 1) * per_z]
        exchange(
            section, 1, "sz", nz,
            lambda t: sum_y.at[section, t],
            lambda d: in_z.at[section, d],
        )
        modal = sum_y[section, sz]
        for d in range(1, nz):
            modal = modal + in_z[section, d]
        return modal

    def spread(section, rows, whole):
        row_out[section] = rows
        exchange(
            section, 2, "sz", nz,
            lambda t: row_out.at[section],
            lambda d: rows_all.at[section, sz],
        )
        rows_all[section, sz] = rows
        block = jnp.concatenate([rows_all[section, z] for z in range(nz)], axis=0).astype(bf16)
        piece[section] = block
        exchange(
            section, 3, "sy", ns,
            lambda t: piece.at[section],
            lambda d: whole.at[my_core, rows_y],
        )
        whole[my_core, rows_y, :] = block

    damping = damping_ref[pl.ds(my_core, 1), :]
    both_halves = coeffs_ref[pl.ds(my_y * per_y + sz * per_z, per_z), :]
    my_rows = jnp.where(my_core == 0, both_halves[:, :half], both_halves[:, half:])

    field_own(state0)
    closure(4, lambda i: (1 + i // 2, 1 + lax.rem(i, 2)))
    halos[2].wait()
    halos[3].wait()
    field_y(state0)
    closure(4, lambda i: (i // 2 * 3, 1 + lax.rem(i, 2)))
    halos[0].wait()
    halos[1].wait()
    field_z(state0)
    closure(8, lambda i: (i // 2, lax.rem(i, 2) * 3))
    project(0)
    first = scale * reduced(0) - damping * my_rows
    middle = my_rows + 0.5 * first
    spread(0, middle, state1)

    field_own(state1)
    field_y(state1)
    field_z(state1)
    closure(16, lambda i: (i // 4, lax.rem(i, 4)))
    project(1)
    second = scale * reduced(1) - damping * middle
    spread(1, 0.5 * (first + second), result)
    out_ref[...] = jnp.concatenate([result[0], result[1]], axis=1).astype(f32)


def local(coeffs, basis, damping, w_in, b_in, w_out):
    batch = coeffs.shape[0]
    modes, rows, depth, width = basis.shape
    ns, nz = lax.axis_size("sy"), lax.axis_size("sz")
    ny = ns // 2
    half = modes // 2
    per_y = batch // ny
    per_z = per_y // nz
    scale = (modes / (rows * depth * width * ns * nz)) ** 0.5
    vmem, smem = pl.BlockSpec(memory_space=pltpu.VMEM), pl.BlockSpec(memory_space=pltpu.SMEM)
    return pl.pallas_call(
        functools.partial(kernel, ny, nz, scale),
        out_shape=jax.ShapeDtypeStruct((batch, modes), f32),
        in_specs=[vmem, vmem, smem, smem, smem, pl.BlockSpec(memory_space=pl.ANY)],
        out_specs=vmem,
        scratch_shapes=[
            pltpu.VMEM((modes * rows * depth, width), bf16),
            pltpu.VMEM((rows, depth, modes, width), bf16),
            pltpu.VMEM((2, depth, modes, width), bf16),
            pltpu.VMEM((2, rows, modes, width), bf16),
            pltpu.VMEM((rows + 2, depth + 2, batch, width), f32),
            pltpu.VMEM((rows, depth, batch, width), f32),
            pltpu.VMEM((rows, depth, batch, width), f32),
            pltpu.VMEM((rows, depth, batch, width), bf16),
            pltpu.VMEM((2, batch, half), bf16),
            pltpu.VMEM((2, batch, half), bf16),
            pltpu.VMEM((2, batch, half), bf16),
            pltpu.VMEM((2, 2, batch, half), f32),
            pltpu.VMEM((2, 2, batch, half), bf16),
            pltpu.VMEM((2, ns, per_y, half), bf16),
            pltpu.VMEM((2, nz, per_z, half), f32),
            pltpu.VMEM((2, nz, per_z, half), f32),
            pltpu.VMEM((2, per_z, half), f32),
            pltpu.VMEM((2, nz, per_z, half), f32),
            pltpu.VMEM((2, per_y, half), bf16),
            pltpu.SemaphoreType.DMA,
            pltpu.SemaphoreType.DMA((4,)),
            pltpu.SemaphoreType.DMA((4,)),
            pltpu.SemaphoreType.DMA((2, 4, 16)),
            pltpu.SemaphoreType.DMA((2, 4, 16)),
        ],
        compiler_params=pltpu.CompilerParams(
            collective_id=0, has_side_effects=True, vmem_limit_bytes=32 << 20
        ),
        cost_estimate=pl.CostEstimate(
            flops=2_000_000_000, bytes_accessed=1_500_000, transcendentals=4_194_304
        ),
    )(
        coeffs, damping.reshape(2, half), w_in, b_in, w_out,
        basis.reshape(modes * rows * depth, width),
    )


def solution(mesh):
    return jax.shard_map(
        local,
        mesh=mesh,
        in_specs=(P("traj", None), P(None, "sy", "sz", None), P(), P(), P(), P()),
        out_specs=P("traj", None),
        check_vma=False,
    )
```

```python
import functools
import jax
import jax.numpy as jnp
from jax import lax
from jax.experimental import pallas as pl
from jax.experimental.pallas import tpu as pltpu
from jax.sharding import PartitionSpec as P

f32, bf16 = jnp.float32, jnp.bfloat16
MESH = pl.DeviceIdType.MESH
CHUNK = 128


def kernel(
    ny, nz, scale,
    coeffs_hbm, damping_hbm, w_in_hbm, b_in_hbm, w_out_hbm, basis_hbm,
    out_ref,
    raw, own, halo_y, halo_z, field, left, right, clos,
    state0, state1, result,
    part_f, part_b, in_y, sum_y, in_z, piece,
    coeffs_ref, damping_ref, w_in, b_in, w_out,
    raw_sem, small_sem, halo_send, halo_recv, send_sem, recv_sem,
):
    ns = 2 * ny
    batch, modes = coeffs_hbm.shape
    half = modes // 2
    per_y = batch // ny
    sy, sz = lax.axis_index("sy"), lax.axis_index("sz")
    my_y, my_core = sy // 2, lax.rem(sy, 2)

    barrier = pltpu.get_barrier_semaphore()

    load = pltpu.make_async_copy(basis_hbm, raw, raw_sem)
    load.start()
    small = [
        pltpu.make_async_copy(src, dst, small_sem.at[i])
        for i, (src, dst) in enumerate((
            (coeffs_hbm, coeffs_ref), (damping_hbm, damping_ref),
            (w_in_hbm, w_in), (b_in_hbm, b_in), (w_out_hbm, w_out),
        ))
    ]
    for copy in small:
        copy.start()

    def greet_y(d, _):
        pl.semaphore_signal(barrier, inc=1, device_id={"sy": lax.rem(sy + d, ns)}, device_id_type=MESH)
        return 0

    def greet_z(d, _):
        pl.semaphore_signal(barrier, inc=1, device_id={"sz": lax.rem(sz + d, nz)}, device_id_type=MESH)
        return 0

    lax.fori_loop(1, ns, greet_y, 0)
    lax.fori_loop(1, nz, greet_z, 0)

    for copy in small:
        copy.wait()
    coeffs = coeffs_ref[...]
    state0[0] = coeffs[:, :half].astype(bf16)
    state0[1] = coeffs[:, half:].astype(bf16)
    source = lax.broadcasted_iota(jnp.int32, (256, 256), 1)
    target = lax.broadcasted_iota(jnp.int32, (256, 256), 0)
    perm = jnp.where(
        (lax.shift_right_logical(target, 4) == (source & 15))
        & ((target & 15) == lax.shift_right_logical(source, 4)),
        1.0, 0.0,
    ).astype(bf16)
    load.wait()
    for block in range(16):
        moved = jnp.dot(
            perm, raw[block * 256:(block + 1) * 256, :], preferred_element_type=f32
        ).astype(bf16)
        for cell in range(16):
            own[cell // 4, cell % 4, block * 16:(block + 1) * 16, :] = moved[cell * 16:(cell + 1) * 16]

    pl.semaphore_wait(barrier, ns + nz - 2)

    y_next, y_prev = lax.rem(sy + 1, ns), lax.rem(sy + ns - 1, ns)
    z_next, z_prev = lax.rem(sz + 1, nz), lax.rem(sz + nz - 1, nz)
    halos = []
    for slot, (src, dst, where) in enumerate((
        (own.at[:, 3], halo_z.at[0], {"sz": z_next}),
        (own.at[:, 0], halo_z.at[1], {"sz": z_prev}),
        (own.at[3], halo_y.at[0], {"sy": y_next}),
        (own.at[0], halo_y.at[1], {"sy": y_prev}),
    )):
        copy = pltpu.make_async_remote_copy(
            src_ref=src, dst_ref=dst, send_sem=halo_send.at[slot], recv_sem=halo_recv.at[slot],
            device_id=where, device_id_type=MESH,
        )
        copy.start()
        halos.append(copy)

    def pair_field(state, first, second):
        lhs = jnp.concatenate([state[0], state[1]], axis=1)
        both = jnp.dot(lhs, jnp.concatenate([first, second], axis=1), preferred_element_type=f32)
        return both[:, :128], both[:, 128:]

    lane = lax.broadcasted_iota(jnp.int32, (batch, 128), 1)

    def field_own(state):
        for y in range(4):
            for z in (0, 2):
                for k, value in enumerate(pair_field(state, own[y, z], own[y, z + 1])):
                    field[y + 1, z + k + 1] = value
                    left[y, z + k] = jnp.where(lane == 0, 0.0, pltpu.roll(value, 1, 1))
                    right[y, z + k] = jnp.where(lane == 127, 0.0, pltpu.roll(value, 127, 1))

    def field_y(state):
        for side, inside in ((0, sy > 0), (1, sy < ns - 1)):
            for z in (0, 2):
                for k, value in enumerate(pair_field(state, halo_y[side, z], halo_y[side, z + 1])):
                    field[5 * side, z + k + 1] = jnp.where(inside, value, 0.0)

    def field_z(state):
        for side, inside in ((0, sz > 0), (1, sz < nz - 1)):
            for y in (0, 2):
                for k, value in enumerate(pair_field(state, halo_z[side, y], halo_z[side, y + 1])):
                    field[y + k + 1, 5 * side] = jnp.where(inside, value, 0.0)

    def closure(count, cell_of):
        chunks = batch // CHUNK

        def body(i, _):
            y, z = cell_of(i // chunks)
            at = pl.ds(pl.multiple_of(lax.rem(i, chunks) * CHUNK, CHUNK), CHUNK)
            taps = (
                field[y + 1, z + 1, at, :],
                field[y, z + 1, at, :],
                field[y + 2, z + 1, at, :],
                left[y, z, at, :],
                right[y, z, at, :],
                field[y + 1, z, at, :],
                field[y + 1, z + 2, at, :],
            )
            total = jnp.zeros((CHUNK, 128), f32)
            for h in range(8):
                inner = b_in[h] + w_in[h, 0] * taps[0]
                for k in range(1, 7):
                    inner = inner + w_in[h, k] * taps[k]
                total = total + w_out[h] * jnp.tanh(inner)
            clos[y, z, at, :] = total.astype(bf16)
            return 0

        lax.fori_loop(0, count * chunks, body, 0)

    def project(section):
        lhs = jnp.concatenate([clos[c // 4, c % 4] for c in range(16)], axis=1)
        rhs = jnp.concatenate([own[c // 4, c % 4] for c in range(16)], axis=1)
        partial = lax.dot_general(lhs, rhs, (((1,), (1,)), ((), ())), preferred_element_type=f32)
        for c in range(2):
            part_f[section, c] = partial[:, c * half:(c + 1) * half]
            part_b[section, c] = partial[:, c * half:(c + 1) * half].astype(bf16)

    def exchange(section, phase, axis, count, src_of, dst_of):
        me = sy if axis == "sy" else sz
        copies = []
        for d in sorted(range(1, count), key=lambda d: -min(d, count - d)):
            peer = lax.rem(me + d, count)
            copy = pltpu.make_async_remote_copy(
                src_ref=src_of(peer), dst_ref=dst_of(d),
                send_sem=send_sem.at[section, phase, d], recv_sem=recv_sem.at[section, phase, d],
                device_id={axis: peer}, device_id_type=MESH,
            )
            copy.start()
            copies.append(copy)
        return copies

    rows_y = pl.ds(pl.multiple_of(my_y * per_y, per_y), per_y)

    def reduced(section):
        copies = exchange(
            section, 0, "sy", ns,
            lambda t: part_b.at[section, lax.rem(t, 2), pl.ds(pl.multiple_of(t // 2 * per_y, per_y), per_y)],
            lambda d: in_y.at[section, d],
        )
        for copy in copies:
            copy.wait()
        total = part_f[section, my_core, rows_y, :]
        for d in range(1, ns):
            total = total + in_y[section, d].astype(f32)
        total = total.astype(bf16)
        sum_y[section] = total
        copies = exchange(
            section, 1, "sz", nz,
            lambda t: sum_y.at[section],
            lambda d: in_z.at[section, sz],
        )
        in_z[section, sz] = total
        for copy in copies:
            copy.wait()
        modal = in_z[section, 0].astype(f32)
        for z in range(1, nz):
            modal = modal + in_z[section, z].astype(f32)
        return modal

    def spread(section, rows, whole):
        block = rows.astype(bf16)
        piece[section] = block
        copies = exchange(
            section, 2, "sy", ns,
            lambda t: piece.at[section],
            lambda d: whole.at[my_core, rows_y],
        )
        whole[my_core, rows_y, :] = block
        for copy in copies:
            copy.wait()

    damping = damping_ref[pl.ds(my_core, 1), :]
    both_halves = coeffs_ref[rows_y, :]
    my_rows = jnp.where(my_core == 0, both_halves[:, :half], both_halves[:, half:])

    field_own(state0)
    closure(4, lambda i: (1 + i // 2, 1 + lax.rem(i, 2)))
    halos[2].wait()
    halos[3].wait()
    field_y(state0)
    closure(4, lambda i: (i // 2 * 3, 1 + lax.rem(i, 2)))
    halos[0].wait()
    halos[1].wait()
    field_z(state0)
    closure(8, lambda i: (i // 2, lax.rem(i, 2) * 3))
    project(0)
    first = scale * reduced(0) - damping * my_rows
    middle = my_rows + 0.5 * first
    spread(0, middle, state1)

    field_own(state1)
    field_y(state1)
    field_z(state1)
    closure(16, lambda i: (i // 4, lax.rem(i, 4)))
    project(1)
    second = scale * reduced(1) - damping * middle
    spread(1, 0.5 * (first + second), result)
    out_ref[...] = jnp.concatenate([result[0], result[1]], axis=1).astype(f32)


def local(coeffs, basis, damping, w_in, b_in, w_out):
    batch = coeffs.shape[0]
    modes, rows, depth, width = basis.shape
    ns, nz = lax.axis_size("sy"), lax.axis_size("sz")
    ny = ns // 2
    half = modes // 2
    per_y = batch // ny
    scale = (modes / (rows * depth * width * ns * nz)) ** 0.5
    return pl.pallas_call(
        functools.partial(kernel, ny, nz, scale),
        out_shape=jax.ShapeDtypeStruct((batch, modes), f32),
        in_specs=[pl.BlockSpec(memory_space=pltpu.HBM)] * 6,
        out_specs=pl.BlockSpec(memory_space=pltpu.VMEM),
        scratch_shapes=[
            pltpu.VMEM((modes * rows * depth, width), bf16),
            pltpu.VMEM((rows, depth, modes, width), bf16),
            pltpu.VMEM((2, depth, modes, width), bf16),
            pltpu.VMEM((2, rows, modes, width), bf16),
            pltpu.VMEM((rows + 2, depth + 2, batch, width), f32),
            pltpu.VMEM((rows, depth, batch, width), f32),
            pltpu.VMEM((rows, depth, batch, width), f32),
            pltpu.VMEM((rows, depth, batch, width), bf16),
            pltpu.VMEM((2, batch, half), bf16),
            pltpu.VMEM((2, batch, half), bf16),
            pltpu.VMEM((2, batch, half), bf16),
            pltpu.VMEM((2, 2, batch, half), f32),
            pltpu.VMEM((2, 2, batch, half), bf16),
            pltpu.VMEM((2, ns, per_y, half), bf16),
            pltpu.VMEM((2, per_y, half), bf16),
            pltpu.VMEM((2, nz, per_y, half), bf16),
            pltpu.VMEM((2, per_y, half), bf16),
            pltpu.VMEM((batch, modes), f32),
            pltpu.VMEM((2, half), f32),
            pltpu.SMEM((8, 7), f32),
            pltpu.SMEM((8,), f32),
            pltpu.SMEM((8,), f32),
            pltpu.SemaphoreType.DMA,
            pltpu.SemaphoreType.DMA((5,)),
            pltpu.SemaphoreType.DMA((4,)),
            pltpu.SemaphoreType.DMA((4,)),
            pltpu.SemaphoreType.DMA((2, 3, 16)),
            pltpu.SemaphoreType.DMA((2, 3, 16)),
        ],
        compiler_params=pltpu.CompilerParams(
            collective_id=0, has_side_effects=True, vmem_limit_bytes=60 << 20
        ),
        cost_estimate=pl.CostEstimate(
            flops=2_000_000_000, bytes_accessed=1_500_000, transcendentals=4_194_304
        ),
    )(
        coeffs, damping.reshape(2, half), w_in, b_in, w_out,
        basis.reshape(modes * rows * depth, width),
    )


def solution(mesh):
    return jax.shard_map(
        local,
        mesh=mesh,
        in_specs=(P("traj", None), P(None, "sy", "sz", None), P(), P(), P(), P()),
        out_specs=P("traj", None),
        check_vma=False,
    )
```

```python
import functools
import jax
import jax.numpy as jnp
from jax import lax
from jax.experimental import pallas as pl
from jax.experimental.pallas import tpu as pltpu
from jax.sharding import PartitionSpec as P

f32, bf16 = jnp.float32, jnp.bfloat16
MESH = pl.DeviceIdType.MESH
GROUP = 4
SUM_TYPE = bf16


def kernel(
    ny, nz, scale,
    coeffs_hbm, damping_hbm, w_in_hbm, b_in_hbm, w_out_hbm, basis_hbm,
    out_ref,
    raw, own, halo_y, halo_z, field, field_b, clos, weights, turned,
    edge_y, edge_z, next_y, next_z,
    state0, state1, result,
    part_f, part_b, in_y, sum_y, in_z, piece,
    coeffs_ref, damping_ref, w_in, b_in, w_out,
    raw_sem, small_sem, halo_send, halo_recv, edge_send, edge_recv, send_sem, recv_sem,
):
    ns = 2 * ny
    batch, modes = coeffs_hbm.shape
    half = modes // 2
    per_y = batch // ny
    sy, sz = lax.axis_index("sy"), lax.axis_index("sz")
    my_y, my_core = sy // 2, lax.rem(sy, 2)

    barrier = pltpu.get_barrier_semaphore()

    load = pltpu.make_async_copy(basis_hbm, raw, raw_sem)
    load.start()
    small = [
        pltpu.make_async_copy(src, dst, small_sem.at[i])
        for i, (src, dst) in enumerate((
            (coeffs_hbm, coeffs_ref), (damping_hbm, damping_ref),
            (w_in_hbm, w_in), (b_in_hbm, b_in), (w_out_hbm, w_out),
        ))
    ]
    for copy in small:
        copy.start()

    def greet_y(d, _):
        pl.semaphore_signal(barrier, inc=1, device_id={"sy": lax.rem(sy + d, ns)}, device_id_type=MESH)
        return 0

    def greet_z(d, _):
        pl.semaphore_signal(barrier, inc=1, device_id={"sz": lax.rem(sz + d, nz)}, device_id_type=MESH)
        return 0

    lax.fori_loop(1, ns, greet_y, 0)
    lax.fori_loop(1, nz, greet_z, 0)

    for copy in small:
        copy.wait()
    coeffs = coeffs_ref[...]
    state0[0] = coeffs[:, :half].astype(bf16)
    state0[1] = coeffs[:, half:].astype(bf16)
    source = lax.broadcasted_iota(jnp.int32, (256, 256), 1)
    target = lax.broadcasted_iota(jnp.int32, (256, 256), 0)
    perm = jnp.where(
        (lax.shift_right_logical(target, 4) == (source & 15))
        & ((target & 15) == lax.shift_right_logical(source, 4)),
        1.0, 0.0,
    ).astype(bf16)
    load.wait()
    for block in range(16):
        moved = jnp.dot(
            perm, raw[block * 256:(block + 1) * 256, :], preferred_element_type=f32
        ).astype(bf16)
        for cell in range(16):
            own[cell // 4, cell % 4, block * 16:(block + 1) * 16, :] = moved[cell * 16:(cell + 1) * 16]

    pl.semaphore_wait(barrier, ns + nz - 2)

    y_next, y_prev = lax.rem(sy + 1, ns), lax.rem(sy + ns - 1, ns)
    z_next, z_prev = lax.rem(sz + 1, nz), lax.rem(sz + nz - 1, nz)
    sides = (({"sz": z_next}, {"sz": z_prev}), ({"sy": y_next}, {"sy": y_prev}))

    def remote(src, dst, send, recv, where):
        return pltpu.make_async_remote_copy(
            src_ref=src, dst_ref=dst, send_sem=send, recv_sem=recv, device_id=where, device_id_type=MESH
        )

    def basis_halo(dim):
        faces = ((own.at[:, 3], own.at[:, 0]), (own.at[3], own.at[0]))[dim]
        copies = [
            remote(
                faces[side], (halo_z, halo_y)[dim].at[side],
                halo_send.at[dim, side], halo_recv.at[dim, side], sides[dim][side],
            )
            for side in range(2)
        ]
        for copy in copies:
            copy.start()
        return copies

    chunks = ns // GROUP
    chunk_rows = batch // chunks
    order = sorted(range(chunks), key=lambda o: (-min(o, chunks - o), o))
    my_chunk, my_place = sy // GROUP, lax.rem(sy, GROUP)

    def chunk_of(offset):
        chunk = lax.rem(my_chunk + offset, chunks)
        return chunk, pl.ds(pl.multiple_of(chunk * chunk_rows, chunk_rows), chunk_rows)

    def edge_copies(offset):
        chunk, at = chunk_of(offset)
        return [
            remote(
                (edge_z, edge_y)[dim].at[side, :, at], (next_z, next_y)[dim].at[side, :, at],
                edge_send.at[dim, side, chunk], edge_recv.at[dim, side, chunk], sides[dim][side],
            )
            for dim in range(2) for side in range(2)
        ]

    def pair_field(state, first, second):
        lhs = jnp.concatenate([state[0], state[1]], axis=1)
        both = jnp.dot(lhs, jnp.concatenate([first, second], axis=1), preferred_element_type=f32)
        return both[:, :128], both[:, 128:]

    def put(y, z, at, value):
        field[y, z, at, :] = value
        if y < 5 and 0 < z < 5:
            field_b[y, z - 1, at, :] = value.astype(bf16)

    everything = slice(None)

    def field_own(state, edges):
        for y in range(4):
            for z in (0, 2):
                for k, value in enumerate(pair_field(state, own[y, z], own[y, z + 1])):
                    put(y + 1, z + k + 1, everything, value)
                    if edges and y in (0, 3):
                        edge_y[int(y == 0), z + k] = value.astype(bf16)
                    if edges and z + k in (0, 3):
                        edge_z[int(z + k == 0), y] = value.astype(bf16)

    def field_y(state):
        for side, inside in ((0, sy > 0), (1, sy < ns - 1)):
            for z in (0, 2):
                for k, value in enumerate(pair_field(state, halo_y[side, z], halo_y[side, z + 1])):
                    put(5 * side, z + k + 1, everything, jnp.where(inside, value, 0.0))

    def field_z(state):
        for side, inside in ((0, sz > 0), (1, sz < nz - 1)):
            for y in (0, 2):
                for k, value in enumerate(pair_field(state, halo_z[side, y], halo_z[side, y + 1])):
                    put(y + k + 1, 5 * side, everything, jnp.where(inside, value, 0.0))

    def edges_in(at):
        for side, inside in ((0, sy > 0), (1, sy < ns - 1)):
            for z in range(4):
                put(5 * side, z + 1, at, jnp.where(inside, next_y[side, z, at, :].astype(f32), 0.0))
        for side, inside in ((0, sz > 0), (1, sz < nz - 1)):
            for y in range(4):
                put(y + 1, 5 * side, at, jnp.where(inside, next_z[side, y, at, :].astype(f32), 0.0))

    def build_weights():
        row = lax.broadcasted_iota(jnp.int32, (128, 128), 0)
        col = lax.broadcasted_iota(jnp.int32, (128, 128), 1)
        for h in range(8):
            band = jnp.where(row == col, w_in[h, 0], 0.0)
            band = jnp.where(row + 1 == col, w_in[h, 3], band)
            band = jnp.where(row == col + 1, w_in[h, 4], band)
            for block, value in enumerate((band, jnp.where(row == col, w_in[h, 1], 0.0))):
                high = value.astype(bf16)
                low = (value - high.astype(f32)).astype(bf16)
                for part, kept in enumerate((high, low)):
                    at = (2 * part + block) * 128
                    weights[at:at + 128, h * 128:(h + 1) * 128] = kept

    def closure(at):
        stack = 128 // chunk_rows

        def body(i, _):
            cells = [((i * stack + j) // 4, lax.rem(i * stack + j, 4)) for j in range(stack)]

            def stacked(take):
                return jnp.concatenate([take(y, z) for y, z in cells], axis=0)

            near = stacked(lambda y, z: jnp.concatenate(
                [field_b[y + 1, z, at, :], field_b[y, z, at, :]], axis=1
            ))
            near = jnp.concatenate([near, near], axis=1)
            taps = (
                (2, stacked(lambda y, z: field[y + 2, z + 1, at, :])),
                (5, stacked(lambda y, z: field[y + 1, z, at, :])),
                (6, stacked(lambda y, z: field[y + 1, z + 2, at, :])),
            )
            total = jnp.zeros((stack * chunk_rows, 128), f32)
            for pair in range(4):
                both = jnp.dot(
                    near, weights[:, pair * 256:(pair + 1) * 256], preferred_element_type=f32
                )
                for k in range(2):
                    h = 2 * pair + k
                    inner = both[:, k * 128:(k + 1) * 128] + b_in[h]
                    for index, tap in taps:
                        inner = inner + w_in[h, index] * tap
                    total = total + w_out[h] * jnp.tanh(inner)
            for j, (y, z) in enumerate(cells):
                clos[y, z, at, :] = total[j * chunk_rows:(j + 1) * chunk_rows].astype(bf16)
            return 0

        lax.fori_loop(0, 16 // stack, body, 0, unroll=4)

    def project(section, offset):
        chunk, at = chunk_of(offset)
        lhs = jnp.concatenate([clos[c // 4, c % 4, at, :] for c in range(16)], axis=1)
        partial = jnp.dot(lhs, turned[...], preferred_element_type=f32)
        for c in range(2):
            part_f[section, c, at, :] = partial[:, c * half:(c + 1) * half]
            part_b[section, c, at, :] = partial[:, c * half:(c + 1) * half].astype(bf16)
        copies = []
        for i in range(int(offset == 0), GROUP):
            place = lax.rem(my_place + i, GROUP) if offset == 0 else i
            target = chunk * GROUP + place
            ahead = lax.rem(target + ns - sy, ns)
            copy = remote(
                part_b.at[section, lax.rem(target, 2), pl.ds(pl.multiple_of(target // 2 * per_y, per_y), per_y)],
                in_y.at[section, ahead],
                send_sem.at[section, 0, offset * GROUP + i], recv_sem.at[section, 0, ahead], {"sy": target},
            )
            copy.start()
            copies.append(copy)
        return copies

    def exchange(section, phase, axis, count, src_of, dst_of):
        me = sy if axis == "sy" else sz
        copies = []
        for d in sorted(range(1, count), key=lambda d: -min(d, count - d)):
            peer = lax.rem(me + d, count)
            copy = pltpu.make_async_remote_copy(
                src_ref=src_of(peer), dst_ref=dst_of(d),
                send_sem=send_sem.at[section, phase, d], recv_sem=recv_sem.at[section, phase, d],
                device_id={axis: peer}, device_id_type=MESH,
            )
            copy.start()
            copies.append(copy)
        return copies

    rows_y = pl.ds(pl.multiple_of(my_y * per_y, per_y), per_y)

    def reduced(section):
        for d in range(1, ns):
            remote(
                piece.at[section], in_y.at[section, d],
                send_sem.at[section, 0, d], recv_sem.at[section, 0, d], {"sy": lax.rem(sy + d, ns)},
            ).wait_recv()
        total = part_f[section, my_core, rows_y, :]
        for d in range(1, ns):
            total = total + in_y[section, d].astype(f32)
        total = total.astype(SUM_TYPE)
        sum_y[section] = total
        copies = exchange(
            section, 1, "sz", nz,
            lambda t: sum_y.at[section],
            lambda d: in_z.at[section, sz],
        )
        between = basis_halo(1) if section == 0 else []
        in_z[section, sz] = total
        for copy in copies:
            copy.wait()
        modal = in_z[section, 0].astype(f32)
        for z in range(1, nz):
            modal = modal + in_z[section, z].astype(f32)
        return modal, between

    def spread(section, rows, whole):
        block = rows.astype(bf16)
        piece[section] = block
        copies = exchange(
            section, 2, "sy", ns,
            lambda t: piece.at[section],
            lambda d: whole.at[my_core, rows_y],
        )
        whole[my_core, rows_y, :] = block
        for copy in copies:
            copy.wait()

    damping = damping_ref[pl.ds(my_core, 1), :]
    both_halves = coeffs_ref[rows_y, :]
    my_rows = jnp.where(my_core == 0, both_halves[:, :half], both_halves[:, half:])

    field_own(state0, True)
    edges = [edge_copies(offset) for offset in order]
    for group in edges:
        for copy in group:
            copy.start()
    build_weights()
    for cell in range(16):
        turned[cell * 128:(cell + 1) * 128, :] = own[cell // 4, cell % 4].T
    sent = []
    for step, offset in enumerate(order):
        for copy in edges[step]:
            copy.wait_recv()
        if step == min(1, chunks - 1):
            halo = basis_halo(0)
        edges_in(chunk_of(offset)[1])
        closure(chunk_of(offset)[1])
        sent += project(0, offset)
    modal, more = reduced(0)
    halo += more
    first = scale * modal - damping * my_rows
    middle = my_rows + 0.5 * first
    spread(0, middle, state1)

    field_own(state1, False)
    for copy in halo:
        copy.wait()
    field_y(state1)
    field_z(state1)
    for offset in order:
        closure(chunk_of(offset)[1])
        sent += project(1, offset)
    modal, _ = reduced(1)
    second = scale * modal - damping * middle
    spread(1, 0.5 * (first + second), result)
    for copy in sum(edges, sent):
        copy.wait_send()
    out_ref[...] = jnp.concatenate([result[0], result[1]], axis=1).astype(f32)


def local(coeffs, basis, damping, w_in, b_in, w_out):
    batch = coeffs.shape[0]
    modes, rows, depth, width = basis.shape
    ns, nz = lax.axis_size("sy"), lax.axis_size("sz")
    ny = ns // 2
    half = modes // 2
    per_y = batch // ny
    scale = (modes / (rows * depth * width * ns * nz)) ** 0.5
    return pl.pallas_call(
        functools.partial(kernel, ny, nz, scale),
        out_shape=jax.ShapeDtypeStruct((batch, modes), f32),
        in_specs=[pl.BlockSpec(memory_space=pltpu.HBM)] * 6,
        out_specs=pl.BlockSpec(memory_space=pltpu.VMEM),
        scratch_shapes=[
            pltpu.VMEM((modes * rows * depth, width), bf16),
            pltpu.VMEM((rows, depth, modes, width), bf16),
            pltpu.VMEM((2, depth, modes, width), bf16),
            pltpu.VMEM((2, rows, modes, width), bf16),
            pltpu.VMEM((rows + 2, depth + 2, batch, width), f32),
            pltpu.VMEM((rows + 1, depth, batch, width), bf16),
            pltpu.VMEM((rows, depth, batch, width), bf16),
            pltpu.VMEM((512, 1024), bf16),
            pltpu.VMEM((rows * depth * width, modes), bf16),
            pltpu.VMEM((2, depth, batch, width), bf16),
            pltpu.VMEM((2, rows, batch, width), bf16),
            pltpu.VMEM((2, depth, batch, width), bf16),
            pltpu.VMEM((2, rows, batch, width), bf16),
            pltpu.VMEM((2, batch, half), bf16),
            pltpu.VMEM((2, batch, half), bf16),
            pltpu.VMEM((2, batch, half), bf16),
            pltpu.VMEM((2, 2, batch, half), f32),
            pltpu.VMEM((2, 2, batch, half), bf16),
            pltpu.VMEM((2, ns, per_y, half), bf16),
            pltpu.VMEM((2, per_y, half), SUM_TYPE),
            pltpu.VMEM((2, nz, per_y, half), SUM_TYPE),
            pltpu.VMEM((2, per_y, half), bf16),
            pltpu.VMEM((batch, modes), f32),
            pltpu.VMEM((2, half), f32),
            pltpu.SMEM((8, 7), f32),
            pltpu.SMEM((8,), f32),
            pltpu.SMEM((8,), f32),
            pltpu.SemaphoreType.DMA,
            pltpu.SemaphoreType.DMA((5,)),
            pltpu.SemaphoreType.DMA((2, 2)),
            pltpu.SemaphoreType.DMA((2, 2)),
            pltpu.SemaphoreType.DMA((2, 2, ns // GROUP)),
            pltpu.SemaphoreType.DMA((2, 2, ns // GROUP)),
            pltpu.SemaphoreType.DMA((2, 3, 16)),
            pltpu.SemaphoreType.DMA((2, 3, 16)),
        ],
        compiler_params=pltpu.CompilerParams(
            collective_id=0, has_side_effects=True, vmem_limit_bytes=60 << 20
        ),
        cost_estimate=pl.CostEstimate(
            flops=2_000_000_000, bytes_accessed=1_500_000, transcendentals=4_194_304
        ),
    )(
        coeffs, damping.reshape(2, half), w_in, b_in, w_out,
        basis.reshape(modes * rows * depth, width),
    )


def solution(mesh):
    return jax.shard_map(
        local,
        mesh=mesh,
        in_specs=(P("traj", None), P(None, "sy", "sz", None), P(), P(), P(), P()),
        out_specs=P("traj", None),
        check_vma=False,
    )
```

```python
import functools
import jax
import jax.numpy as jnp
from jax import lax
from jax.experimental import pallas as pl
from jax.experimental.pallas import tpu as pltpu
from jax.sharding import PartitionSpec as P

f32, bf16 = jnp.float32, jnp.bfloat16
MESH = pl.DeviceIdType.MESH
GROUP = 4
SUM_TYPE = bf16


def kernel(
    ny, nz, scale,
    coeffs_hbm, damping_hbm, w_in_hbm, b_in_hbm, w_out_hbm, basis_hbm,
    out_ref,
    raw, own, halo_y, halo_z, field, field_b, clos, weights, turned,
    edge_y, edge_z, next_y, next_z,
    state0, state1, result,
    part_f, part_b, in_y, sum_y, in_z, piece,
    coeffs_ref, damping_ref, w_in, b_in, w_out,
    raw_sem, small_sem, halo_send, halo_recv, edge_send, edge_recv, send_sem, recv_sem,
):
    ns = 2 * ny
    batch, modes = coeffs_hbm.shape
    half = modes // 2
    per_y = batch // ny
    sy, sz = lax.axis_index("sy"), lax.axis_index("sz")
    my_y, my_core = sy // 2, lax.rem(sy, 2)

    barrier = pltpu.get_barrier_semaphore()

    part = raw.shape[0] // 4
    loads = [
        pltpu.make_async_copy(
            basis_hbm.at[i * part:(i + 1) * part], raw.at[i * part:(i + 1) * part], raw_sem.at[i]
        )
        for i in range(4)
    ]
    for copy in loads:
        copy.start()
    small = [
        pltpu.make_async_copy(src, dst, small_sem.at[i])
        for i, (src, dst) in enumerate((
            (coeffs_hbm, coeffs_ref), (damping_hbm, damping_ref),
            (w_in_hbm, w_in), (b_in_hbm, b_in), (w_out_hbm, w_out),
        ))
    ]
    for copy in small:
        copy.start()

    def greet_y(d, _):
        pl.semaphore_signal(barrier, inc=1, device_id={"sy": lax.rem(sy + d, ns)}, device_id_type=MESH)
        return 0

    def greet_z(d, _):
        pl.semaphore_signal(barrier, inc=1, device_id={"sz": lax.rem(sz + d, nz)}, device_id_type=MESH)
        return 0

    lax.fori_loop(1, ns, greet_y, 0)
    lax.fori_loop(1, nz, greet_z, 0)

    for copy in small:
        copy.wait()
    coeffs = coeffs_ref[...]
    state0[0] = coeffs[:, :half].astype(bf16)
    state0[1] = coeffs[:, half:].astype(bf16)
    source = lax.broadcasted_iota(jnp.int32, (256, 256), 1)
    target = lax.broadcasted_iota(jnp.int32, (256, 256), 0)
    perm = jnp.where(
        (lax.shift_right_logical(target, 4) == (source & 15))
        & ((target & 15) == lax.shift_right_logical(source, 4)),
        1.0, 0.0,
    ).astype(bf16)
    for block in range(16):
        if block % 4 == 0:
            loads[block // 4].wait()
        moved = jnp.dot(
            perm, raw[block * 256:(block + 1) * 256, :], preferred_element_type=f32
        ).astype(bf16)
        for cell in range(16):
            own[cell // 4, cell % 4, block * 16:(block + 1) * 16, :] = moved[cell * 16:(cell + 1) * 16]

    pl.semaphore_wait(barrier, ns + nz - 2)

    y_next, y_prev = lax.rem(sy + 1, ns), lax.rem(sy + ns - 1, ns)
    z_next, z_prev = lax.rem(sz + 1, nz), lax.rem(sz + nz - 1, nz)
    sides = (({"sz": z_next}, {"sz": z_prev}), ({"sy": y_next}, {"sy": y_prev}))

    def remote(src, dst, send, recv, where):
        return pltpu.make_async_remote_copy(
            src_ref=src, dst_ref=dst, send_sem=send, recv_sem=recv, device_id=where, device_id_type=MESH
        )

    def basis_halo(dim):
        faces = ((own.at[:, 3], own.at[:, 0]), (own.at[3], own.at[0]))[dim]
        copies = [
            remote(
                faces[side], (halo_z, halo_y)[dim].at[side],
                halo_send.at[dim, side], halo_recv.at[dim, side], sides[dim][side],
            )
            for side in range(2)
        ]
        for copy in copies:
            copy.start()
        return copies

    chunks = ns // GROUP
    chunk_rows = batch // chunks
    order = sorted(range(chunks), key=lambda o: (-min(o, chunks - o), o))
    my_chunk, my_place = sy // GROUP, lax.rem(sy, GROUP)

    def chunk_of(offset):
        chunk = lax.rem(my_chunk + offset, chunks)
        return chunk, pl.ds(pl.multiple_of(chunk * chunk_rows, chunk_rows), chunk_rows)

    def edge_copies(offset):
        chunk, at = chunk_of(offset)
        return [
            remote(
                (edge_z, edge_y)[dim].at[side, :, at], (next_z, next_y)[dim].at[side, :, at],
                edge_send.at[dim, side, chunk], edge_recv.at[dim, side, chunk], sides[dim][side],
            )
            for dim in range(2) for side in range(2)
        ]

    def pair_field(state, first, second):
        lhs = jnp.concatenate([state[0], state[1]], axis=1)
        both = jnp.dot(lhs, jnp.concatenate([first, second], axis=1), preferred_element_type=f32)
        return both[:, :128], both[:, 128:]

    def put(y, z, at, value):
        field[y, z, at, :] = value
        if y < 5 and 0 < z < 5:
            field_b[y, z - 1, at, :] = value.astype(bf16)

    everything = slice(None)

    def field_own(state, edges):
        for y in range(4):
            for z in (0, 2):
                for k, value in enumerate(pair_field(state, own[y, z], own[y, z + 1])):
                    put(y + 1, z + k + 1, everything, value)
                    if edges and y in (0, 3):
                        edge_y[int(y == 0), z + k] = value.astype(bf16)
                    if edges and z + k in (0, 3):
                        edge_z[int(z + k == 0), y] = value.astype(bf16)

    def field_y(state):
        for side, inside in ((0, sy > 0), (1, sy < ns - 1)):
            for z in (0, 2):
                for k, value in enumerate(pair_field(state, halo_y[side, z], halo_y[side, z + 1])):
                    put(5 * side, z + k + 1, everything, jnp.where(inside, value, 0.0))

    def field_z(state):
        for side, inside in ((0, sz > 0), (1, sz < nz - 1)):
            for y in (0, 2):
                for k, value in enumerate(pair_field(state, halo_z[side, y], halo_z[side, y + 1])):
                    put(y + k + 1, 5 * side, everything, jnp.where(inside, value, 0.0))

    def edges_in(at):
        for side, inside in ((0, sy > 0), (1, sy < ns - 1)):
            for z in range(4):
                put(5 * side, z + 1, at, jnp.where(inside, next_y[side, z, at, :].astype(f32), 0.0))
        for side, inside in ((0, sz > 0), (1, sz < nz - 1)):
            for y in range(4):
                put(y + 1, 5 * side, at, jnp.where(inside, next_z[side, y, at, :].astype(f32), 0.0))

    def build_weights():
        row = lax.broadcasted_iota(jnp.int32, (128, 128), 0)
        col = lax.broadcasted_iota(jnp.int32, (128, 128), 1)
        for h in range(8):
            band = jnp.where(row == col, w_in[h, 0], 0.0)
            band = jnp.where(row + 1 == col, w_in[h, 3], band)
            band = jnp.where(row == col + 1, w_in[h, 4], band)
            for block, value in enumerate((band, jnp.where(row == col, w_in[h, 1], 0.0))):
                high = value.astype(bf16)
                low = (value - high.astype(f32)).astype(bf16)
                for part, kept in enumerate((high, low)):
                    at = (2 * part + block) * 128
                    weights[at:at + 128, h * 128:(h + 1) * 128] = kept

    inner_cells = [(1, 1), (1, 2), (2, 1), (2, 2)]
    outer_cells = [(y, z) for y in range(4) for z in range(4) if (y, z) not in inner_cells]
    stack = 128 // chunk_rows

    def closure(at, listed):
        for first_of in range(0, len(listed), stack):
            cells = listed[first_of:first_of + stack]

            def stacked(take):
                return jnp.concatenate([take(y, z) for y, z in cells], axis=0)

            near = stacked(lambda y, z: jnp.concatenate(
                [field_b[y + 1, z, at, :], field_b[y, z, at, :]], axis=1
            ))
            near = jnp.concatenate([near, near], axis=1)
            taps = (
                (2, stacked(lambda y, z: field[y + 2, z + 1, at, :])),
                (5, stacked(lambda y, z: field[y + 1, z, at, :])),
                (6, stacked(lambda y, z: field[y + 1, z + 2, at, :])),
            )
            total = jnp.zeros((stack * chunk_rows, 128), f32)
            for pair in range(4):
                both = jnp.dot(
                    near, weights[:, pair * 256:(pair + 1) * 256], preferred_element_type=f32
                )
                for k in range(2):
                    h = 2 * pair + k
                    inner = both[:, k * 128:(k + 1) * 128] + b_in[h]
                    for index, tap in taps:
                        inner = inner + w_in[h, index] * tap
                    total = total + w_out[h] * jnp.tanh(inner)
            for j, (y, z) in enumerate(cells):
                clos[y, z, at, :] = total[j * chunk_rows:(j + 1) * chunk_rows].astype(bf16)

    def project(section, offset):
        chunk, at = chunk_of(offset)
        lhs = jnp.concatenate([clos[c // 4, c % 4, at, :] for c in range(16)], axis=1)
        partial = jnp.dot(lhs, turned[...], preferred_element_type=f32)
        for c in range(2):
            part_f[section, c, at, :] = partial[:, c * half:(c + 1) * half]
            part_b[section, c, at, :] = partial[:, c * half:(c + 1) * half].astype(bf16)
        copies = []
        for i in range(int(offset == 0), GROUP):
            place = lax.rem(my_place + i, GROUP) if offset == 0 else i
            target = chunk * GROUP + place
            ahead = lax.rem(target + ns - sy, ns)
            copy = remote(
                part_b.at[section, lax.rem(target, 2), pl.ds(pl.multiple_of(target // 2 * per_y, per_y), per_y)],
                in_y.at[section, ahead],
                send_sem.at[section, 0, offset * GROUP + i], recv_sem.at[section, 0, ahead], {"sy": target},
            )
            copy.start()
            copies.append(copy)
        return copies

    def exchange(section, phase, axis, count, src_of, dst_of):
        me = sy if axis == "sy" else sz
        copies = []
        for d in sorted(range(1, count), key=lambda d: -min(d, count - d)):
            peer = lax.rem(me + d, count)
            copy = pltpu.make_async_remote_copy(
                src_ref=src_of(peer), dst_ref=dst_of(d),
                send_sem=send_sem.at[section, phase, d], recv_sem=recv_sem.at[section, phase, d],
                device_id={axis: peer}, device_id_type=MESH,
            )
            copy.start()
            copies.append(copy)
        return copies

    rows_y = pl.ds(pl.multiple_of(my_y * per_y, per_y), per_y)

    def reduced(section):
        for d in range(1, ns):
            remote(
                piece.at[section], in_y.at[section, d],
                send_sem.at[section, 0, d], recv_sem.at[section, 0, d], {"sy": lax.rem(sy + d, ns)},
            ).wait_recv()
        total = part_f[section, my_core, rows_y, :]
        for d in range(1, ns):
            total = total + in_y[section, d].astype(f32)
        total = total.astype(SUM_TYPE)
        sum_y[section] = total
        copies = exchange(
            section, 1, "sz", nz,
            lambda t: sum_y.at[section],
            lambda d: in_z.at[section, sz],
        )
        between = basis_halo(1) if section == 0 else []
        in_z[section, sz] = total
        for copy in copies:
            copy.wait()
        modal = in_z[section, 0].astype(f32)
        for z in range(1, nz):
            modal = modal + in_z[section, z].astype(f32)
        return modal, between

    def spread(section, rows, whole):
        block = rows.astype(bf16)
        piece[section] = block
        copies = exchange(
            section, 2, "sy", ns,
            lambda t: piece.at[section],
            lambda d: whole.at[my_core, rows_y],
        )
        whole[my_core, rows_y, :] = block
        for copy in copies:
            copy.wait()

    damping = damping_ref[pl.ds(my_core, 1), :]
    both_halves = coeffs_ref[rows_y, :]
    my_rows = jnp.where(my_core == 0, both_halves[:, :half], both_halves[:, half:])

    field_own(state0, True)
    edges = [edge_copies(offset) for offset in order]
    for group in edges:
        for copy in group:
            copy.start()
    build_weights()
    for cell in range(16):
        turned[cell * 128:(cell + 1) * 128, :] = own[cell // 4, cell % 4].T
    for offset in order:
        closure(chunk_of(offset)[1], inner_cells)
    sent = []
    for step, offset in enumerate(order):
        for copy in edges[step]:
            copy.wait_recv()
        if step == min(1, chunks - 1):
            halo = basis_halo(0)
        edges_in(chunk_of(offset)[1])
        closure(chunk_of(offset)[1], outer_cells)
        sent += project(0, offset)
    modal, more = reduced(0)
    halo += more
    first = scale * modal - damping * my_rows
    middle = my_rows + 0.5 * first
    spread(0, middle, state1)

    field_own(state1, False)
    for copy in halo:
        copy.wait()
    field_y(state1)
    field_z(state1)
    for offset in order:
        closure(chunk_of(offset)[1], inner_cells + outer_cells)
        sent += project(1, offset)
    modal, _ = reduced(1)
    second = scale * modal - damping * middle
    spread(1, 0.5 * (first + second), result)
    for copy in sum(edges, sent):
        copy.wait_send()
    out_ref[...] = jnp.concatenate([result[0], result[1]], axis=1).astype(f32)


def local(coeffs, basis, damping, w_in, b_in, w_out):
    batch = coeffs.shape[0]
    modes, rows, depth, width = basis.shape
    ns, nz = lax.axis_size("sy"), lax.axis_size("sz")
    ny = ns // 2
    half = modes // 2
    per_y = batch // ny
    scale = (modes / (rows * depth * width * ns * nz)) ** 0.5
    return pl.pallas_call(
        functools.partial(kernel, ny, nz, scale),
        out_shape=jax.ShapeDtypeStruct((batch, modes), f32),
        in_specs=[pl.BlockSpec(memory_space=pltpu.HBM)] * 6,
        out_specs=pl.BlockSpec(memory_space=pltpu.VMEM),
        scratch_shapes=[
            pltpu.VMEM((modes * rows * depth, width), bf16),
            pltpu.VMEM((rows, depth, modes, width), bf16),
            pltpu.VMEM((2, depth, modes, width), bf16),
            pltpu.VMEM((2, rows, modes, width), bf16),
            pltpu.VMEM((rows + 2, depth + 2, batch, width), f32),
            pltpu.VMEM((rows + 1, depth, batch, width), bf16),
            pltpu.VMEM((rows, depth, batch, width), bf16),
            pltpu.VMEM((512, 1024), bf16),
            pltpu.VMEM((rows * depth * width, modes), bf16),
            pltpu.VMEM((2, depth, batch, width), bf16),
            pltpu.VMEM((2, rows, batch, width), bf16),
            pltpu.VMEM((2, depth, batch, width), bf16),
            pltpu.VMEM((2, rows, batch, width), bf16),
            pltpu.VMEM((2, batch, half), bf16),
            pltpu.VMEM((2, batch, half), bf16),
            pltpu.VMEM((2, batch, half), bf16),
            pltpu.VMEM((2, 2, batch, half), f32),
            pltpu.VMEM((2, 2, batch, half), bf16),
            pltpu.VMEM((2, ns, per_y, half), bf16),
            pltpu.VMEM((2, per_y, half), SUM_TYPE),
            pltpu.VMEM((2, nz, per_y, half), SUM_TYPE),
            pltpu.VMEM((2, per_y, half), bf16),
            pltpu.VMEM((batch, modes), f32),
            pltpu.VMEM((2, half), f32),
            pltpu.SMEM((8, 7), f32),
            pltpu.SMEM((8,), f32),
            pltpu.SMEM((8,), f32),
            pltpu.SemaphoreType.DMA((4,)),
            pltpu.SemaphoreType.DMA((5,)),
            pltpu.SemaphoreType.DMA((2, 2)),
            pltpu.SemaphoreType.DMA((2, 2)),
            pltpu.SemaphoreType.DMA((2, 2, ns // GROUP)),
            pltpu.SemaphoreType.DMA((2, 2, ns // GROUP)),
            pltpu.SemaphoreType.DMA((2, 3, 16)),
            pltpu.SemaphoreType.DMA((2, 3, 16)),
        ],
        compiler_params=pltpu.CompilerParams(
            collective_id=0, has_side_effects=True, vmem_limit_bytes=60 << 20
        ),
        cost_estimate=pl.CostEstimate(
            flops=2_000_000_000, bytes_accessed=1_500_000, transcendentals=4_194_304
        ),
    )(
        coeffs, damping.reshape(2, half), w_in, b_in, w_out,
        basis.reshape(modes * rows * depth, width),
    )


def solution(mesh):
    return jax.shard_map(
        local,
        mesh=mesh,
        in_specs=(P("traj", None), P(None, "sy", "sz", None), P(), P(), P(), P()),
        out_specs=P("traj", None),
        check_vma=False,
    )
```

```python
import functools
import jax
import jax.numpy as jnp
from jax import lax
from jax.experimental import pallas as pl
from jax.experimental.pallas import tpu as pltpu
from jax.sharding import PartitionSpec as P

f32, bf16 = jnp.float32, jnp.bfloat16
MESH = pl.DeviceIdType.MESH
GROUP = 4
SUM_TYPE = bf16


def kernel(
    ny, nz, scale,
    coeffs_hbm, damping_hbm, w_in_hbm, b_in_hbm, w_out_hbm, basis_hbm,
    out_ref,
    raw, own, halo_y, halo_z, field, field_b, clos, weights, turned,
    edge_y, edge_z, next_y, next_z,
    state0, state1, result,
    part_f, part_b, in_y, sum_y, in_z, piece,
    coeffs_ref, damping_ref, w_in, b_in, w_out,
    raw_sem, small_sem, halo_send, halo_recv, edge_send, edge_recv, send_sem, recv_sem,
):
    ns = 2 * ny
    batch, modes = coeffs_hbm.shape
    half = modes // 2
    per_y = batch // ny
    sy, sz = lax.axis_index("sy"), lax.axis_index("sz")
    my_y, my_core = sy // 2, lax.rem(sy, 2)

    barrier = pltpu.get_barrier_semaphore()

    part = raw.shape[0] // 4
    loads = [
        pltpu.make_async_copy(
            basis_hbm.at[i * part:(i + 1) * part], raw.at[i * part:(i + 1) * part], raw_sem.at[i]
        )
        for i in range(4)
    ]
    for copy in loads:
        copy.start()
    small = [
        pltpu.make_async_copy(src, dst, small_sem.at[i])
        for i, (src, dst) in enumerate((
            (coeffs_hbm, coeffs_ref), (damping_hbm, damping_ref),
            (w_in_hbm, w_in), (b_in_hbm, b_in), (w_out_hbm, w_out),
        ))
    ]
    for copy in small:
        copy.start()

    def greet_y(d, _):
        pl.semaphore_signal(barrier, inc=1, device_id={"sy": lax.rem(sy + d, ns)}, device_id_type=MESH)
        return 0

    def greet_z(d, _):
        pl.semaphore_signal(barrier, inc=1, device_id={"sz": lax.rem(sz + d, nz)}, device_id_type=MESH)
        return 0

    lax.fori_loop(1, ns, greet_y, 0)
    lax.fori_loop(1, nz, greet_z, 0)

    for copy in small:
        copy.wait()
    coeffs = coeffs_ref[...]
    state0[0] = coeffs[:, :half].astype(bf16)
    state0[1] = coeffs[:, half:].astype(bf16)
    source = lax.broadcasted_iota(jnp.int32, (256, 256), 1)
    target = lax.broadcasted_iota(jnp.int32, (256, 256), 0)
    perm = jnp.where(
        (lax.shift_right_logical(target, 4) == (source & 15))
        & ((target & 15) == lax.shift_right_logical(source, 4)),
        1.0, 0.0,
    ).astype(bf16)
    for block in range(16):
        if block % 4 == 0:
            loads[block // 4].wait()
        moved = jnp.dot(
            perm, raw[block * 256:(block + 1) * 256, :], preferred_element_type=f32
        ).astype(bf16)
        for cell in range(16):
            own[cell // 4, cell % 4, block * 16:(block + 1) * 16, :] = moved[cell * 16:(cell + 1) * 16]

    pl.semaphore_wait(barrier, ns + nz - 2)

    y_next, y_prev = lax.rem(sy + 1, ns), lax.rem(sy + ns - 1, ns)
    z_next, z_prev = lax.rem(sz + 1, nz), lax.rem(sz + nz - 1, nz)
    sides = (({"sz": z_next}, {"sz": z_prev}), ({"sy": y_next}, {"sy": y_prev}))

    def remote(src, dst, send, recv, where):
        return pltpu.make_async_remote_copy(
            src_ref=src, dst_ref=dst, send_sem=send, recv_sem=recv, device_id=where, device_id_type=MESH
        )

    def basis_halo(dim):
        faces = ((own.at[:, 3], own.at[:, 0]), (own.at[3], own.at[0]))[dim]
        copies = [
            remote(
                faces[side], (halo_z, halo_y)[dim].at[side],
                halo_send.at[dim, side], halo_recv.at[dim, side], sides[dim][side],
            )
            for side in range(2)
        ]
        for copy in copies:
            copy.start()
        return copies

    chunks = ns // GROUP
    chunk_rows = batch // chunks
    order = [*range(1, chunks), 0]
    my_chunk, my_place = sy // GROUP, lax.rem(sy, GROUP)

    def chunk_of(offset):
        chunk = lax.rem(my_chunk + offset, chunks)
        return chunk, pl.ds(pl.multiple_of(chunk * chunk_rows, chunk_rows), chunk_rows)

    def edge_copies(offset):
        chunk, at = chunk_of(offset)
        return [
            remote(
                (edge_z, edge_y)[dim].at[side, :, at], (next_z, next_y)[dim].at[side, :, at],
                edge_send.at[dim, side, chunk], edge_recv.at[dim, side, chunk], sides[dim][side],
            )
            for dim in range(2) for side in range(2)
        ]

    def pair_field(state, at, first, second):
        lhs = jnp.concatenate([state[0, at, :], state[1, at, :]], axis=1)
        both = jnp.dot(lhs, jnp.concatenate([first, second], axis=1), preferred_element_type=f32)
        return both[:, :128], both[:, 128:]

    def put(y, z, at, value):
        field[y, z, at, :] = value
        if y < 5 and 0 < z < 5:
            field_b[y, z - 1, at, :] = value.astype(bf16)

    everything = slice(None)

    def field_own(state, at, edges):
        for y in range(4):
            for z in (0, 2):
                for k, value in enumerate(pair_field(state, at, own[y, z], own[y, z + 1])):
                    put(y + 1, z + k + 1, at, value)
                    if edges and y in (0, 3):
                        edge_y[int(y == 0), z + k] = value.astype(bf16)
                    if edges and z + k in (0, 3):
                        edge_z[int(z + k == 0), y] = value.astype(bf16)

    def field_y(state, at):
        for side, inside in ((0, sy > 0), (1, sy < ns - 1)):
            for z in (0, 2):
                for k, value in enumerate(pair_field(state, at, halo_y[side, z], halo_y[side, z + 1])):
                    put(5 * side, z + k + 1, at, jnp.where(inside, value, 0.0))

    def field_z(state, at):
        for side, inside in ((0, sz > 0), (1, sz < nz - 1)):
            for y in (0, 2):
                for k, value in enumerate(pair_field(state, at, halo_z[side, y], halo_z[side, y + 1])):
                    put(y + k + 1, 5 * side, at, jnp.where(inside, value, 0.0))

    def edges_in(at):
        for side, inside in ((0, sy > 0), (1, sy < ns - 1)):
            for z in range(4):
                put(5 * side, z + 1, at, jnp.where(inside, next_y[side, z, at, :].astype(f32), 0.0))
        for side, inside in ((0, sz > 0), (1, sz < nz - 1)):
            for y in range(4):
                put(y + 1, 5 * side, at, jnp.where(inside, next_z[side, y, at, :].astype(f32), 0.0))

    def build_weights():
        row = lax.broadcasted_iota(jnp.int32, (128, 128), 0)
        col = lax.broadcasted_iota(jnp.int32, (128, 128), 1)
        for h in range(8):
            band = jnp.where(row == col, w_in[h, 0], 0.0)
            band = jnp.where(row + 1 == col, w_in[h, 3], band)
            band = jnp.where(row == col + 1, w_in[h, 4], band)
            for block, value in enumerate((band, jnp.where(row == col, w_in[h, 1], 0.0))):
                high = value.astype(bf16)
                low = (value - high.astype(f32)).astype(bf16)
                for part, kept in enumerate((high, low)):
                    at = (2 * part + block) * 128
                    weights[at:at + 128, h * 128:(h + 1) * 128] = kept

    inner_cells = [(1, 1), (1, 2), (2, 1), (2, 2)]
    outer_cells = [(y, z) for y in range(4) for z in range(4) if (y, z) not in inner_cells]
    stack = 128 // chunk_rows

    def closure(at, listed):
        for first_of in range(0, len(listed), stack):
            cells = listed[first_of:first_of + stack]

            def stacked(take):
                return jnp.concatenate([take(y, z) for y, z in cells], axis=0)

            near = stacked(lambda y, z: jnp.concatenate(
                [field_b[y + 1, z, at, :], field_b[y, z, at, :]], axis=1
            ))
            near = jnp.concatenate([near, near], axis=1)
            taps = (
                (2, stacked(lambda y, z: field[y + 2, z + 1, at, :])),
                (5, stacked(lambda y, z: field[y + 1, z, at, :])),
                (6, stacked(lambda y, z: field[y + 1, z + 2, at, :])),
            )
            total = jnp.zeros((stack * chunk_rows, 128), f32)
            for pair in range(4):
                both = jnp.dot(
                    near, weights[:, pair * 256:(pair + 1) * 256], preferred_element_type=f32
                )
                for k in range(2):
                    h = 2 * pair + k
                    inner = both[:, k * 128:(k + 1) * 128] + b_in[h]
                    for index, tap in taps:
                        inner = inner + w_in[h, index] * tap
                    total = total + w_out[h] * jnp.tanh(inner)
            for j, (y, z) in enumerate(cells):
                clos[y, z, at, :] = total[j * chunk_rows:(j + 1) * chunk_rows].astype(bf16)

    def project(section, offset):
        chunk, at = chunk_of(offset)
        lhs = jnp.concatenate([clos[c // 4, c % 4, at, :] for c in range(16)], axis=1)
        partial = jnp.dot(lhs, turned[...], preferred_element_type=f32)
        for c in range(2):
            part_f[section, c, at, :] = partial[:, c * half:(c + 1) * half]
            part_b[section, c, at, :] = partial[:, c * half:(c + 1) * half].astype(bf16)
        copies = []
        for i in range(int(offset == 0), GROUP):
            place = lax.rem(my_place + i, GROUP) if offset == 0 else i
            target = chunk * GROUP + place
            ahead = lax.rem(target + ns - sy, ns)
            copy = remote(
                part_b.at[section, lax.rem(target, 2), pl.ds(pl.multiple_of(target // 2 * per_y, per_y), per_y)],
                in_y.at[section, ahead],
                send_sem.at[section, 0, offset * GROUP + i], recv_sem.at[section, 0, ahead], {"sy": target},
            )
            copy.start()
            copies.append(copy)
        return copies

    pending = []

    def exchange(section, phase, axis, count, src_of, dst_of):
        me = sy if axis == "sy" else sz
        copies = []
        for d in sorted(range(1, count), key=lambda d: -min(d, count - d)):
            peer = lax.rem(me + d, count)
            copy = pltpu.make_async_remote_copy(
                src_ref=src_of(peer), dst_ref=dst_of(d),
                send_sem=send_sem.at[section, phase, d], recv_sem=recv_sem.at[section, phase, d],
                device_id={axis: peer}, device_id_type=MESH,
            )
            copy.start()
            copies.append(copy)
        while pending:
            pending.pop().wait_send()
        pending.extend(copies)
        return copies[::-1]

    rows_y = pl.ds(pl.multiple_of(my_y * per_y, per_y), per_y)

    def reduced(section):
        total = part_f[section, my_core, rows_y, :]
        for d in sorted(range(1, ns), key=lambda d: -min(d, ns - d)):
            remote(
                piece.at[section], in_y.at[section, d],
                send_sem.at[section, 0, d], recv_sem.at[section, 0, d], {"sy": lax.rem(sy + d, ns)},
            ).wait_recv()
            total = total + in_y[section, d].astype(f32)
        total = total.astype(SUM_TYPE)
        sum_y[section] = total
        copies = exchange(
            section, 1, "sz", nz,
            lambda t: sum_y.at[section],
            lambda d: in_z.at[section, sz],
        )
        between = basis_halo(1) if section == 0 else []
        in_z[section, sz] = total
        for copy in copies:
            copy.wait_recv()
        modal = in_z[section, 0].astype(f32)
        for z in range(1, nz):
            modal = modal + in_z[section, z].astype(f32)
        return modal, between

    def spread(section, rows, whole):
        block = rows.astype(bf16)
        piece[section] = block
        copies = exchange(
            section, 2, "sy", ns,
            lambda t: piece.at[section],
            lambda d: whole.at[my_core, rows_y],
        )
        whole[my_core, rows_y, :] = block
        return copies

    def gathered(section, offset):
        chunk, _ = chunk_of(offset)
        for i in range(int(offset == 0), GROUP):
            source = chunk * GROUP + (lax.rem(my_place + i, GROUP) if offset == 0 else i)
            behind = lax.rem(sy + ns - source, ns)
            remote(
                sum_y.at[section], piece.at[section],
                send_sem.at[section, 2, behind], recv_sem.at[section, 2, behind], {"sy": source},
            ).wait_recv()

    damping = damping_ref[pl.ds(my_core, 1), :]
    both_halves = coeffs_ref[rows_y, :]
    my_rows = jnp.where(my_core == 0, both_halves[:, :half], both_halves[:, half:])

    field_own(state0, everything, True)
    edges = [edge_copies(offset) for offset in order]
    for group in edges:
        for copy in group:
            copy.start()
    build_weights()
    for cell in range(16):
        turned[cell * 128:(cell + 1) * 128, :] = own[cell // 4, cell % 4].T
    for offset in order:
        closure(chunk_of(offset)[1], inner_cells)
    pending.extend(sum(edges, []))
    for step, offset in enumerate(order):
        for copy in edges[step]:
            copy.wait_recv()
        if step == min(1, chunks - 1):
            halo = basis_halo(0)
        edges_in(chunk_of(offset)[1])
        closure(chunk_of(offset)[1], outer_cells)
        pending.extend(project(0, offset))
    modal, more = reduced(0)
    halo += more
    first = scale * modal - damping * my_rows
    middle = my_rows + 0.5 * first
    spread(0, middle, state1)

    for copy in halo:
        copy.wait_recv()
    pending.extend(halo)
    for step, offset in enumerate(order):
        if step < 2:
            for chunk in order[:1] if step == 0 else order[1:]:
                gathered(0, chunk)
            at = chunk_of(offset)[1] if step == 0 else everything
            field_own(state1, at, False)
            field_y(state1, at)
            field_z(state1, at)
        closure(chunk_of(offset)[1], inner_cells + outer_cells)
        pending.extend(project(1, offset))
    modal, _ = reduced(1)
    second = scale * modal - damping * middle
    for copy in spread(1, 0.5 * (first + second), result):
        copy.wait_recv()
    while pending:
        pending.pop().wait_send()
    out_ref[...] = jnp.concatenate([result[0], result[1]], axis=1).astype(f32)


def local(coeffs, basis, damping, w_in, b_in, w_out):
    batch = coeffs.shape[0]
    modes, rows, depth, width = basis.shape
    ns, nz = lax.axis_size("sy"), lax.axis_size("sz")
    ny = ns // 2
    half = modes // 2
    per_y = batch // ny
    scale = (modes / (rows * depth * width * ns * nz)) ** 0.5
    return pl.pallas_call(
        functools.partial(kernel, ny, nz, scale),
        out_shape=jax.ShapeDtypeStruct((batch, modes), f32),
        in_specs=[pl.BlockSpec(memory_space=pltpu.HBM)] * 6,
        out_specs=pl.BlockSpec(memory_space=pltpu.VMEM),
        scratch_shapes=[
            pltpu.VMEM((modes * rows * depth, width), bf16),
            pltpu.VMEM((rows, depth, modes, width), bf16),
            pltpu.VMEM((2, depth, modes, width), bf16),
            pltpu.VMEM((2, rows, modes, width), bf16),
            pltpu.VMEM((rows + 2, depth + 2, batch, width), f32),
            pltpu.VMEM((rows + 1, depth, batch, width), bf16),
            pltpu.VMEM((rows, depth, batch, width), bf16),
            pltpu.VMEM((512, 1024), bf16),
            pltpu.VMEM((rows * depth * width, modes), bf16),
            pltpu.VMEM((2, depth, batch, width), bf16),
            pltpu.VMEM((2, rows, batch, width), bf16),
            pltpu.VMEM((2, depth, batch, width), bf16),
            pltpu.VMEM((2, rows, batch, width), bf16),
            pltpu.VMEM((2, batch, half), bf16),
            pltpu.VMEM((2, batch, half), bf16),
            pltpu.VMEM((2, batch, half), bf16),
            pltpu.VMEM((2, 2, batch, half), f32),
            pltpu.VMEM((2, 2, batch, half), bf16),
            pltpu.VMEM((2, ns, per_y, half), bf16),
            pltpu.VMEM((2, per_y, half), SUM_TYPE),
            pltpu.VMEM((2, nz, per_y, half), SUM_TYPE),
            pltpu.VMEM((2, per_y, half), bf16),
            pltpu.VMEM((batch, modes), f32),
            pltpu.VMEM((2, half), f32),
            pltpu.SMEM((8, 7), f32),
            pltpu.SMEM((8,), f32),
            pltpu.SMEM((8,), f32),
            pltpu.SemaphoreType.DMA((4,)),
            pltpu.SemaphoreType.DMA((5,)),
            pltpu.SemaphoreType.DMA((2, 2)),
            pltpu.SemaphoreType.DMA((2, 2)),
            pltpu.SemaphoreType.DMA((2, 2, ns // GROUP)),
            pltpu.SemaphoreType.DMA((2, 2, ns // GROUP)),
            pltpu.SemaphoreType.DMA((2, 3, 16)),
            pltpu.SemaphoreType.DMA((2, 3, 16)),
        ],
        compiler_params=pltpu.CompilerParams(
            collective_id=0, has_side_effects=True, vmem_limit_bytes=60 << 20
        ),
        cost_estimate=pl.CostEstimate(
            flops=2_000_000_000, bytes_accessed=1_500_000, transcendentals=4_194_304
        ),
    )(
        coeffs, damping.reshape(2, half), w_in, b_in, w_out,
        basis.reshape(modes * rows * depth, width),
    )


def solution(mesh):
    return jax.shard_map(
        local,
        mesh=mesh,
        in_specs=(P("traj", None), P(None, "sy", "sz", None), P(), P(), P(), P()),
        out_specs=P("traj", None),
        check_vma=False,
    )
```
